32 devices in a mesh: freq: 8 (over z, core), src: 4 (over y, x).
Axes of the slice: x: 2, y: 2, z: 4, core: 2. Of those that a mesh axis runs over, the one named last changes fastest.
Arguments:
- reflection: bfloat16 [8, 2, 6400, 6400], P('freq', None, 'src'), may hold values from -0.078125 to 0.078125
- f_zero: float32 [8, 2, 16, 6400], P('freq'), may hold values from -6 to 6
- onset: int32 [16, 6400], replicated, may hold values from 64 to 447
Outputs:
- f_plus: float32 [8, 2, 16, 6400], P('freq')
- f_minus: float32 [8, 2, 16, 6400], P('freq', None, None, 'src')
The draws below stay inside these ranges and needn't reach their ends.
All inputs are finite; a program needn't handle non-finite values.
Results may differ from the reference program's by a relative error of at most 0.013.
Values may be sent and summed in bfloat16 or wider, within the bound.
A program may use at most 192 MiB of HBM per device.

```python
import math
import jax
import jax.numpy as jnp
from jax import lax

POINTS = 6400
SAMPLES = 512
VIRTUAL = 16
LOW_BIN = 4
ROUNDS = 5
FREQS = 8


def with_ends(drawn, stream_key, low, top_value):
    shape = drawn.shape
    place = [jax.random.randint(jax.random.fold_in(stream_key, axis), (), 0, shape[axis]) for axis in range(len(shape))]
    drawn = drawn.at[tuple(place)].set(low)
    longest = shape.index(max(shape))
    place[longest] = (place[longest] + 1) % shape[longest]
    return drawn.at[tuple(place)].set(top_value)


def levels(own_key, dims, cuts, least, high):
    def one(position, parts):
        steps = jax.random.uniform(jax.random.fold_in(jax.random.fold_in(own_key, 6), position), (parts,), jnp.float32, least / len(cuts), high / len(cuts))
        return jnp.repeat(jnp.exp(steps), dims[position] // parts).reshape((-1,) + (1,) * (len(dims) - position - 1))

    gain = one(*cuts[0])
    for cut in cuts[1:]:
        gain = gain * one(*cut)
    return gain


def normal_values(rng, dims, deviation, reach, split=(), held_as=jnp.bfloat16):
    values = jax.random.normal(rng, dims, jnp.float32) * deviation
    if len(split) > 0:
        values = levels(rng, dims, split, -0.22, 0.18) * values
    return jnp.clip(values, min=-reach, max=reach).astype(held_as)


def setup_inputs(seed: int = 0) -> dict:
    splits = jax.random.split(jax.random.key(seed), 4)
    reflection = normal_values(splits[0], (FREQS, 2, POINTS, POINTS), POINTS ** -0.5, 0.078125, ((0, 8), (2, 4)))
    f_zero = normal_values(splits[1], (FREQS, 2, VIRTUAL, POINTS), 1.0, 6.0, ((0, 8),), jnp.float32)
    onset = with_ends(jax.random.randint(splits[2], (VIRTUAL, POINTS), SAMPLES // 8, SAMPLES - SAMPLES // 8), jax.random.fold_in(splits[2], 1), SAMPLES // 8, (SAMPLES - SAMPLES // 8) - 1).astype(jnp.int32)
    return dict(reflection=reflection, f_zero=f_zero, onset=onset)


def band_table(count, samples):
    bins = lax.broadcasted_iota(jnp.int32, (count, samples), 0) + (LOW_BIN + 1)
    moments = lax.broadcasted_iota(jnp.int32, (count, samples), 1)
    phase = (bins * moments % samples).astype(jnp.float32) * (2.0 * math.pi / samples)
    factor = math.sqrt(2.0 / samples)
    return jnp.stack([factor * jnp.cos(phase), -factor * jnp.sin(phase)], axis=1).reshape(2 * count, samples)

def windowed(spectra, onset, table):
    flat = spectra.reshape(2 * FREQS, VIRTUAL * POINTS)
    traces = jnp.einsum('an,at->nt', flat, table, precision=lax.Precision.HIGHEST)
    moments = lax.broadcasted_iota(jnp.int32, traces.shape, 1)
    kept = jnp.where(moments < onset.reshape(VIRTUAL * POINTS, 1), traces, jnp.zeros_like(traces))
    back = jnp.einsum('at,nt->an', table, kept, precision=lax.Precision.HIGHEST)
    return back.reshape(FREQS, 2, VIRTUAL, POINTS)

def forward_one(pair):
    refl, plus_b = pair
    prod = jnp.dot(plus_b.reshape(2 * VIRTUAL, POINTS), refl.reshape(2 * POINTS, POINTS).T, preferred_element_type=jnp.float32).reshape(2, VIRTUAL, 2, POINTS)
    real = prod[0, :, 0] - prod[1, :, 1]
    imag = prod[1, :, 0] + prod[0, :, 1]
    return jnp.stack([real, imag])

def adjoint_one(pair):
    refl, minus_b = pair
    flat = minus_b.reshape(2 * VIRTUAL, POINTS)
    first = jnp.dot(flat, refl[0], preferred_element_type=jnp.float32).reshape(2, VIRTUAL, POINTS)
    second = jnp.dot(flat, refl[1], preferred_element_type=jnp.float32).reshape(2, VIRTUAL, POINTS)
    real = first[0] + second[1]
    imag = first[1] - second[0]
    return jnp.stack([real, imag])

def reference(reflection, f_zero, onset):
    table = band_table(FREQS, SAMPLES)
    plus = f_zero
    f_minus = f_zero
    for step in range(ROUNDS):
        plus_b = plus.astype(jnp.bfloat16)
        records = lax.map(forward_one, (reflection, plus_b))
        f_minus = windowed(records, onset, table)
        minus_b = f_minus.astype(jnp.bfloat16)
        traces = lax.map(adjoint_one, (reflection, minus_b))
        plus = f_zero + windowed(traces, onset, table)
    return (plus, f_minus)
```

```python
import functools
import math

import jax
import jax.numpy as jnp
import ml_dtypes
import numpy as np
from jax import lax
from jax.experimental import pallas as pl
from jax.experimental.pallas import tpu as pltpu
from jax.sharding import PartitionSpec as P

SAMPLES = 512
LOW_BIN = 4
ROUNDS = 5
LANES = 128
TILE = 256
MESH = pl.DeviceIdType.MESH


def round_up(value, unit):
    return -(-value // unit) * unit


def starts(total, count, width):
    return [min(width * k, total - width) for k in range(count)]


def band_table(count):
    bins = np.arange(count)[:, None] + (LOW_BIN + 1)
    moments = np.arange(SAMPLES)[None, :]
    phase = (bins * moments % SAMPLES) * (2.0 * math.pi / SAMPLES)
    factor = math.sqrt(2.0 / SAMPLES)
    return np.stack([factor * np.cos(phase), -factor * np.sin(phase)], axis=1).reshape(
        2 * count, SAMPLES
    )


def kernel(
    n_freq,
    n_src,
    refl_hbm,
    zero_ref,
    onset_src_ref,
    onset_recv_ref,
    spread_ref,
    gather_ref,
    plus_ref,
    minus_ref,
    refl,
    lhs,
    mlhs,
    rec,
    acc,
    snd,
    got1,
    got2,
    part_snd,
    got3,
    got4,
    got5,
    piece,
    got6,
    load_sem,
    send_sem,
    recv_sem,
):
    me_f = lax.axis_index("freq")
    me_s = lax.axis_index("src")
    rows, points = refl.shape[1], refl.shape[2]
    two_v = lhs.shape[1]
    virt = two_v // 2
    wide = piece.shape[1]
    narrow = snd.shape[2]
    wide_starts = starts(points, n_src, wide)
    narrow_starts = starts(wide, n_freq, narrow)
    edges = list(range(0, rows, TILE))

    def load(j, start, size):
        return pltpu.make_async_copy(
            refl_hbm.at[0, :, pl.ds(start, size), :],
            refl.at[:, pl.ds(start, size), :],
            load_sem.at[j],
        )

    for j, start in enumerate(edges):
        load(j, start, min(TILE, rows - start)).start()

    barrier = pltpu.get_barrier_semaphore()
    for d in range(1, n_freq):
        pl.semaphore_signal(
            barrier, inc=1, device_id={"freq": lax.rem(me_f + d, n_freq)}, device_id_type=MESH
        )
    for d in range(1, n_src):
        pl.semaphore_signal(
            barrier, inc=1, device_id={"src": lax.rem(me_s + d, n_src)}, device_id_type=MESH
        )
    pl.semaphore_wait(barrier, n_freq + n_src - 2)

    def exchange(phase, axis, count, me, source, target):
        copies = []
        for d in range(1, count):
            peer = lax.rem(me + d, count)
            copy = pltpu.make_async_remote_copy(
                src_ref=source(peer),
                dst_ref=target.at[me],
                send_sem=send_sem.at[phase, d],
                recv_sem=recv_sem.at[phase, d],
                device_id={axis: peer},
                device_id_type=MESH,
            )
            copy.start()
            copies.append(copy)
        target[me] = source(me)[...]
        for copy in copies:
            copy.wait()

    def window(source, onset_ref, target):
        spectra = source[...].reshape(n_freq * two_v, narrow)
        row = lax.broadcasted_iota(jnp.int32, (n_freq * two_v, narrow), 0) % virt
        moment = lax.broadcasted_iota(jnp.int32, (SAMPLES, narrow), 0)

        def one(v, total):
            mine = row == v
            picked = jnp.where(mine, spectra.astype(jnp.float32), 0.0).astype(jnp.bfloat16)
            traces = jnp.dot(spread_ref[...], picked, preferred_element_type=jnp.float32)
            kept = jnp.where(moment < onset_ref[pl.ds(v, 1), :], traces, 0.0).astype(jnp.bfloat16)
            back = jnp.dot(gather_ref[...], kept, preferred_element_type=jnp.float32)
            return jnp.where(mine, back, total)

        total = lax.fori_loop(
            0, virt, one, jnp.zeros((n_freq * two_v, narrow), jnp.float32), unroll=2
        )
        target[...] = total.astype(jnp.bfloat16).reshape(n_freq, two_v, narrow)

    def set_plus(values):
        low = values.astype(jnp.bfloat16)
        lhs[0] = low
        lhs[1, :virt] = (-values[virt:]).astype(jnp.bfloat16)
        lhs[1, virt:] = values[:virt].astype(jnp.bfloat16)

    set_plus(zero_ref[0].reshape(two_v, points))
    rec[...] = jnp.zeros_like(rec)

    def forward(start, size):
        out = None
        for p in range(2):
            term = lax.dot_general(
                lhs[p],
                refl[p, pl.ds(start, size), :],
                (((1,), (1,)), ((), ())),
                preferred_element_type=jnp.float32,
            )
            out = term if out is None else out + term
        return out

    def round_body(step, carry):
        full = rows // TILE

        def forward_tile(j, c):
            start = pl.multiple_of(j * TILE, TILE)

            @pl.when(step == 0)
            def _():
                load(j, start, TILE).wait()

            rec[:, pl.ds(start, TILE)] = forward(start, TILE)
            return c

        lax.fori_loop(0, full, forward_tile, 0)
        if rows % TILE:
            start, size = full * TILE, rows % TILE

            @pl.when(step == 0)
            def _():
                load(full, start, size).wait()

            rec[:, start : start + size] = forward(start, size)
        for k in range(n_freq):
            at = narrow_starts[k]
            snd[k] = rec[:, at : at + narrow].astype(jnp.bfloat16)
        exchange(0, "freq", n_freq, me_f, lambda k: snd.at[k], got1)
        window(got1, onset_src_ref, snd)
        exchange(1, "freq", n_freq, me_f, lambda k: snd.at[k], got2)
        for k in range(n_freq):
            at = narrow_starts[k]
            block = got2[k]
            mlhs[0, :, at : at + narrow] = block
            value = block.astype(jnp.float32)
            mlhs[1, :virt, at : at + narrow] = block[virt:]
            mlhs[1, virt:, at : at + narrow] = (-value[:virt]).astype(jnp.bfloat16)
        minus_ref[0] = mlhs[0, :, :rows].astype(jnp.float32).reshape(2, virt, rows)

        def adjoint_tile(j, c):
            columns = pl.ds(pl.multiple_of(j * TILE, TILE), TILE)
            out = None
            for p in range(2):
                term = jnp.dot(
                    mlhs[p, :, :rows], refl[p, :, columns], preferred_element_type=jnp.float32
                )
                out = term if out is None else out + term
            acc[:, columns] = out.astype(jnp.bfloat16)
            return c

        lax.fori_loop(0, points // TILE, adjoint_tile, 0)
        for k in range(n_src):
            at = wide_starts[k]
            part_snd[k] = acc[:, at : at + wide]
        exchange(2, "src", n_src, me_s, lambda k: part_snd.at[k], got3)
        total = got3[0].astype(jnp.float32)
        for k in range(1, n_src):
            total = total + got3[k].astype(jnp.float32)
        low = total.astype(jnp.bfloat16)
        for k in range(n_freq):
            at = narrow_starts[k]
            snd[k] = low[:, at : at + narrow]
        exchange(3, "freq", n_freq, me_f, lambda k: snd.at[k], got4)
        window(got4, onset_recv_ref, snd)
        exchange(4, "freq", n_freq, me_f, lambda k: snd.at[k], got5)
        for k in range(n_freq):
            at = narrow_starts[k]
            piece[:, at : at + narrow] = got5[k]
        exchange(5, "src", n_src, me_s, lambda k: piece, got6)
        for k in range(n_src):
            at = wide_starts[k]
            zero = zero_ref[0, :, :, at : at + wide].reshape(two_v, wide)
            plus = zero + got6[k].astype(jnp.float32)
            plus_ref[0, :, :, at : at + wide] = plus.reshape(2, virt, wide)
            lhs[0, :, at : at + wide] = plus.astype(jnp.bfloat16)
            lhs[1, :virt, at : at + wide] = (-plus[virt:]).astype(jnp.bfloat16)
            lhs[1, virt:, at : at + wide] = plus[:virt].astype(jnp.bfloat16)
        return carry

    lax.fori_loop(0, ROUNDS, round_body, 0)


def body(reflection, f_zero, onset):
    n_freq = lax.axis_size("freq")
    n_src = lax.axis_size("src")
    freq_index = lax.axis_index("freq")
    src_index = lax.axis_index("src")
    _, _, rows, points = reflection.shape
    virt = f_zero.shape[2]
    two_v = 2 * virt
    wide = round_up(rows, LANES)
    narrow = round_up(-(-wide // n_freq), LANES)
    narrow_start = jnp.minimum(freq_index * narrow, wide - narrow)
    own = lax.dynamic_slice_in_dim(onset, src_index * rows, rows, 1)
    onset_src = lax.dynamic_slice_in_dim(
        jnp.pad(own, ((0, 0), (0, wide - rows))), narrow_start, narrow, 1
    )
    onset_recv = lax.dynamic_slice_in_dim(
        onset, jnp.minimum(src_index * wide, points - wide) + narrow_start, narrow, 1
    )
    table = np.repeat(band_table(n_freq), virt, axis=0).astype(ml_dtypes.bfloat16)
    gather = jnp.asarray(table)
    spread = jnp.asarray(np.ascontiguousarray(table.T))
    low = jnp.bfloat16
    vmem = pl.BlockSpec(memory_space=pltpu.VMEM)
    exchange_shape = pltpu.VMEM((n_freq, two_v, narrow), low)
    piece_shape = pltpu.VMEM((n_src, two_v, wide), low)
    return pl.pallas_call(
        functools.partial(kernel, n_freq, n_src),
        out_shape=(
            jax.ShapeDtypeStruct(f_zero.shape, jnp.float32),
            jax.ShapeDtypeStruct((1, 2, virt, rows), jnp.float32),
        ),
        in_specs=[pl.BlockSpec(memory_space=pl.ANY)] + [vmem] * 5,
        out_specs=(vmem, vmem),
        scratch_shapes=[
            pltpu.VMEM((2, rows, points), low),
            pltpu.VMEM((2, two_v, points), low),
            pltpu.VMEM((2, two_v, wide), low),
            pltpu.VMEM((two_v, wide), jnp.float32),
            pltpu.VMEM((two_v, points), low),
            exchange_shape,
            exchange_shape,
            exchange_shape,
            piece_shape,
            piece_shape,
            exchange_shape,
            exchange_shape,
            pltpu.VMEM((two_v, wide), low),
            piece_shape,
            pltpu.SemaphoreType.DMA((-(-rows // TILE),)),
            pltpu.SemaphoreType.DMA((6, max(n_freq, n_src))),
            pltpu.SemaphoreType.DMA((6, max(n_freq, n_src))),
        ],
        compiler_params=pltpu.CompilerParams(
            collective_id=0, has_side_effects=True, vmem_limit_bytes=60 * 2**20
        ),
    )(reflection, f_zero, onset_src, onset_recv, spread, gather)


def solution(mesh):
    return jax.shard_map(
        body,
        mesh=mesh,
        in_specs=(P("freq", None, "src", None), P("freq", None, None, None), P()),
        out_specs=(P("freq", None, None, None), P("freq", None, None, "src")),
        check_vma=False,
    )
```

```python
import functools
import math

import jax
import jax.numpy as jnp
import ml_dtypes
import numpy as np
from jax import lax
from jax.experimental import pallas as pl
from jax.experimental.pallas import tpu as pltpu
from jax.sharding import PartitionSpec as P

SAMPLES = 512
LOW_BIN = 4
ROUNDS = 5
LANES = 128
TILE = 256
MESH = pl.DeviceIdType.MESH


def round_up(value, unit):
    return -(-value // unit) * unit


def starts(total, count, width):
    return [min(width * k, total - width) for k in range(count)]


def band_table(count):
    bins = np.arange(count)[:, None] + (LOW_BIN + 1)
    moments = np.arange(SAMPLES)[None, :]
    phase = (bins * moments % SAMPLES) * (2.0 * math.pi / SAMPLES)
    factor = math.sqrt(2.0 / SAMPLES)
    return np.stack([factor * np.cos(phase), -factor * np.sin(phase)], axis=1).reshape(
        2 * count, SAMPLES
    )


def kernel(
    n_freq,
    n_src,
    refl_hbm,
    zero_ref,
    onset_src_ref,
    onset_recv_ref,
    spread_ref,
    gather_ref,
    plus_ref,
    minus_ref,
    refl,
    lhs,
    mlhs,
    rec,
    snd,
    got1,
    got2,
    part_snd,
    got3,
    got4,
    got5,
    piece,
    got6,
    load_sem,
    send_sem,
    recv_sem,
):
    me_f = lax.axis_index("freq")
    me_s = lax.axis_index("src")
    rows, points = refl.shape[1], refl.shape[2]
    two_v = lhs.shape[1]
    virt = two_v // 2
    wide = piece.shape[1]
    narrow = snd.shape[2]
    wide_starts = starts(points, n_src, wide)
    narrow_starts = starts(wide, n_freq, narrow)
    edges = list(range(0, rows, TILE))

    def load(j, start, size):
        return pltpu.make_async_copy(
            refl_hbm.at[0, :, pl.ds(start, size), :],
            refl.at[:, pl.ds(start, size), :],
            load_sem.at[j],
        )

    for j, start in enumerate(edges):
        load(j, start, min(TILE, rows - start)).start()

    barrier = pltpu.get_barrier_semaphore()
    for d in range(1, n_freq):
        pl.semaphore_signal(
            barrier, inc=1, device_id={"freq": lax.rem(me_f + d, n_freq)}, device_id_type=MESH
        )
    for d in range(1, n_src):
        pl.semaphore_signal(
            barrier, inc=1, device_id={"src": lax.rem(me_s + d, n_src)}, device_id_type=MESH
        )
    pl.semaphore_wait(barrier, n_freq + n_src - 2)

    def exchange(phase, axis, count, me, source, target):
        copies = []
        for d in range(1, count):
            peer = lax.rem(me + d, count)
            copy = pltpu.make_async_remote_copy(
                src_ref=source(peer),
                dst_ref=target.at[me],
                send_sem=send_sem.at[phase, d],
                recv_sem=recv_sem.at[phase, d],
                device_id={axis: peer},
                device_id_type=MESH,
            )
            copy.start()
            copies.append(copy)
        target[me] = source(me)[...]
        for copy in copies:
            copy.wait()

    def window(source, onset_ref, target):
        spectra = source[...].reshape(n_freq * two_v, narrow)
        row = lax.broadcasted_iota(jnp.int32, (n_freq * two_v, narrow), 0) % virt
        moment = lax.broadcasted_iota(jnp.int32, (SAMPLES, narrow), 0)

        def one(v, total):
            mine = row == v
            picked = jnp.where(mine, spectra.astype(jnp.float32), 0.0).astype(jnp.bfloat16)
            traces = jnp.dot(spread_ref[...], picked, preferred_element_type=jnp.float32)
            kept = jnp.where(moment < onset_ref[pl.ds(v, 1), :], traces, 0.0).astype(jnp.bfloat16)
            back = jnp.dot(gather_ref[...], kept, preferred_element_type=jnp.float32)
            return jnp.where(mine, back, total)

        total = lax.fori_loop(
            0, virt, one, jnp.zeros((n_freq * two_v, narrow), jnp.float32), unroll=16
        )
        target[...] = total.astype(jnp.bfloat16).reshape(n_freq, two_v, narrow)

    def set_plus(values):
        low = values.astype(jnp.bfloat16)
        lhs[0] = low
        lhs[1, :virt] = (-values[virt:]).astype(jnp.bfloat16)
        lhs[1, virt:] = values[:virt].astype(jnp.bfloat16)

    set_plus(zero_ref[0].reshape(two_v, points))
    rec[...] = jnp.zeros_like(rec)

    def forward(start, size):
        out = None
        for p in range(2):
            term = lax.dot_general(
                refl[p, pl.ds(start, size), :],
                lhs[p],
                (((1,), (1,)), ((), ())),
                preferred_element_type=jnp.float32,
            )
            out = term if out is None else out + term
        return out.T

    def round_body(step, carry):
        full = rows // TILE

        def to_freq(k, slot):
            return pltpu.make_async_remote_copy(
                src_ref=snd.at[k],
                dst_ref=got1.at[slot],
                send_sem=send_sem.at[0, k],
                recv_sem=recv_sem.at[0, slot],
                device_id={"freq": k},
                device_id_type=MESH,
            )

        def send_records(k, block):
            snd[k] = block.astype(jnp.bfloat16)

            @pl.when(k != me_f)
            def _():
                to_freq(k, me_f).start()

        each = TILE // narrow

        def forward_tile(j, c):
            start = pl.multiple_of(j * TILE, TILE)

            @pl.when(step == 0)
            def _():
                load(j, start, TILE).wait()

            out = forward(start, TILE)
            rec[:, pl.ds(start, TILE)] = out
            for i in range(each):
                send_records(j * each + i, out[:, i * narrow : (i + 1) * narrow])
            return c

        lax.fori_loop(0, full, forward_tile, 0)
        if rows % TILE:
            start, size = full * TILE, rows % TILE

            @pl.when(step == 0)
            def _():
                load(full, start, size).wait()

            rec[:, start : start + size] = forward(start, size)
        for k in range(full * each, n_freq):
            at = narrow_starts[k]
            send_records(k, rec[:, at : at + narrow])
        got1[me_f] = snd[me_f]
        for d in range(1, n_freq):
            k = lax.rem(me_f + d, n_freq)
            to_freq(k, k).wait()
        window(got1, onset_src_ref, snd)
        exchange(1, "freq", n_freq, me_f, lambda k: snd.at[k], got2)
        for k in range(n_freq):
            at = narrow_starts[k]
            block = got2[k]
            mlhs[0, :, at : at + narrow] = block
            value = block.astype(jnp.float32)
            mlhs[1, :virt, at : at + narrow] = block[virt:]
            mlhs[1, virt:, at : at + narrow] = (-value[:virt]).astype(jnp.bfloat16)
        minus_ref[0] = mlhs[0, :, :rows].astype(jnp.float32).reshape(2, virt, rows)

        def to_src(d):
            peer = lax.rem(me_s + d, n_src)
            return pltpu.make_async_remote_copy(
                src_ref=part_snd.at[peer],
                dst_ref=got3.at[me_s],
                send_sem=send_sem.at[2, d],
                recv_sem=recv_sem.at[2, d],
                device_id={"src": peer},
                device_id_type=MESH,
            )

        def adjoint(peer):
            start = peer * wide - (peer // (n_src - 1)) * (n_src * wide - points)
            columns = pl.ds(pl.multiple_of(start, LANES), wide)
            out = None
            for p in range(2):
                term = jnp.dot(
                    mlhs[p, :, :rows], refl[p, :, columns], preferred_element_type=jnp.float32
                )
                out = term if out is None else out + term
            part_snd[peer] = out.astype(jnp.bfloat16)

        def adjoint_piece(d, c):
            adjoint(lax.rem(me_s + d, n_src))

            @pl.when(d < n_src)
            def _():
                to_src(d).start()

            return c

        lax.fori_loop(1, n_src + 1, adjoint_piece, 0)
        got3[me_s] = part_snd[me_s]
        for d in range(1, n_src):
            to_src(d).wait()
        total = got3[0].astype(jnp.float32)
        for k in range(1, n_src):
            total = total + got3[k].astype(jnp.float32)
        low = total.astype(jnp.bfloat16)
        for k in range(n_freq):
            at = narrow_starts[k]
            snd[k] = low[:, at : at + narrow]
        exchange(3, "freq", n_freq, me_f, lambda k: snd.at[k], got4)
        window(got4, onset_recv_ref, snd)
        exchange(4, "freq", n_freq, me_f, lambda k: snd.at[k], got5)
        for k in range(n_freq):
            at = narrow_starts[k]
            piece[:, at : at + narrow] = got5[k]
        exchange(5, "src", n_src, me_s, lambda k: piece, got6)
        for k in range(n_src):
            at = wide_starts[k]
            zero = zero_ref[0, :, :, at : at + wide].reshape(two_v, wide)
            plus = zero + got6[k].astype(jnp.float32)
            plus_ref[0, :, :, at : at + wide] = plus.reshape(2, virt, wide)
            lhs[0, :, at : at + wide] = plus.astype(jnp.bfloat16)
            lhs[1, :virt, at : at + wide] = (-plus[virt:]).astype(jnp.bfloat16)
            lhs[1, virt:, at : at + wide] = plus[:virt].astype(jnp.bfloat16)
        return carry

    lax.fori_loop(0, ROUNDS, round_body, 0)


def body(reflection, f_zero, onset):
    n_freq = lax.axis_size("freq")
    n_src = lax.axis_size("src")
    freq_index = lax.axis_index("freq")
    src_index = lax.axis_index("src")
    _, _, rows, points = reflection.shape
    virt = f_zero.shape[2]
    two_v = 2 * virt
    wide = round_up(rows, LANES)
    narrow = round_up(-(-wide // n_freq), LANES)
    narrow_start = jnp.minimum(freq_index * narrow, wide - narrow)
    own = lax.dynamic_slice_in_dim(onset, src_index * rows, rows, 1)
    onset_src = lax.dynamic_slice_in_dim(
        jnp.pad(own, ((0, 0), (0, wide - rows))), narrow_start, narrow, 1
    )
    onset_recv = lax.dynamic_slice_in_dim(
        onset, jnp.minimum(src_index * wide, points - wide) + narrow_start, narrow, 1
    )
    table = np.repeat(band_table(n_freq), virt, axis=0).astype(ml_dtypes.bfloat16)
    gather = jnp.asarray(table)
    spread = jnp.asarray(np.ascontiguousarray(table.T))
    low = jnp.bfloat16
    vmem = pl.BlockSpec(memory_space=pltpu.VMEM)
    exchange_shape = pltpu.VMEM((n_freq, two_v, narrow), low)
    piece_shape = pltpu.VMEM((n_src, two_v, wide), low)
    return pl.pallas_call(
        functools.partial(kernel, n_freq, n_src),
        out_shape=(
            jax.ShapeDtypeStruct(f_zero.shape, jnp.float32),
            jax.ShapeDtypeStruct((1, 2, virt, rows), jnp.float32),
        ),
        in_specs=[pl.BlockSpec(memory_space=pl.ANY)] + [vmem] * 5,
        out_specs=(vmem, vmem),
        scratch_shapes=[
            pltpu.VMEM((2, rows, points), low),
            pltpu.VMEM((2, two_v, points), low),
            pltpu.VMEM((2, two_v, wide), low),
            pltpu.VMEM((two_v, wide), jnp.float32),
            exchange_shape,
            exchange_shape,
            exchange_shape,
            piece_shape,
            piece_shape,
            exchange_shape,
            exchange_shape,
            pltpu.VMEM((two_v, wide), low),
            piece_shape,
            pltpu.SemaphoreType.DMA((-(-rows // TILE),)),
            pltpu.SemaphoreType.DMA((6, max(n_freq, n_src))),
            pltpu.SemaphoreType.DMA((6, max(n_freq, n_src))),
        ],
        compiler_params=pltpu.CompilerParams(
            collective_id=0, has_side_effects=True, vmem_limit_bytes=60 * 2**20
        ),
    )(reflection, f_zero, onset_src, onset_recv, spread, gather)


def solution(mesh):
    return jax.shard_map(
        body,
        mesh=mesh,
        in_specs=(P("freq", None, "src", None), P("freq", None, None, None), P()),
        out_specs=(P("freq", None, None, None), P("freq", None, None, "src")),
        check_vma=False,
    )
```
